256 devices in a mesh: row: 8 (over y, core), col: 32 (over z, x).
Axes of the slice: x: 4, y: 4, z: 8, core: 2. Of those that a mesh axis runs over, the one named last changes fastest.
Arguments:
- gradient: bfloat16 [9216, 36864], P(('row', 'col')), may hold values from -140 to 140
- weights: float32 [9216, 36864], P('row', 'col'), may hold values from -0.06 to 0.06
- row_old: float32 [9216], P(('row', 'col')), may hold values from 0.02 to 40, as said below
- col_old: float32 [36864], P('col'), may hold values from 0.02 to 40, as said below
Outputs:
- new_weights: float32 [9216, 36864], P('row', 'col')
- row_moment: float32 [9216], P(('row', 'col'))
- col_moment: float32 [36864], P('col')
The draws below stay inside these ranges and needn't reach their ends.
Inputs may be any that keep to these rules, and one draw needn't show every extreme that they name: `row_old`: positive. `col_old`: positive.
All inputs are finite; a program needn't handle non-finite values.
Results may differ from the reference program's by a relative error of at most 0.0003.
Values may be sent and summed in bfloat16 or wider, within the bound.
A program may use at most 64 MiB of HBM per device.

```python
import math
import jax
import jax.numpy as jnp
from jax import lax

D = 9216
FF = 36864


def shared_scales(key):
    row_scale = jnp.exp(jax.random.uniform(jax.random.fold_in(key, 101), (D,), jnp.float32, math.log(0.3), math.log(2.0)))
    col_scale = jnp.exp(jax.random.uniform(jax.random.fold_in(key, 102), (FF,), jnp.float32, math.log(0.3), math.log(2.0)))
    return (row_scale, col_scale)


def draw_gradient(key, part):
    row_scale, col_scale = shared_scales(key)
    key = jax.random.fold_in(key, 1)
    table_key = jax.random.fold_in(key, 7)
    noise_key = jax.random.fold_in(key, 8)
    noise = jnp.clip(jax.random.normal(noise_key, (D, FF), jnp.float32), -5.0, 5.0)
    block_table = jnp.exp(jax.random.uniform(table_key, (8, 8), jnp.float32, math.log(0.5), math.log(2.0)))
    row_block = jnp.arange(D, dtype=jnp.int32) * 8 // D
    col_block = jnp.arange(FF, dtype=jnp.int32) * 8 // FF
    amplitude = block_table[row_block[:, None], col_block[None, :]]
    row_ramp = 3.0 ** (0.5 * jnp.arange(D, dtype=jnp.float32) / (D - 1))
    col_ramp = 3.0 ** (0.5 * jnp.arange(FF, dtype=jnp.float32) / (FF - 1))
    return (noise * amplitude * (row_scale * row_ramp)[:, None] * (col_scale * col_ramp)[None, :]).astype(jnp.bfloat16)


def draw_row_old(key, part):
    row_scale, col_scale = shared_scales(key)
    key = jax.random.fold_in(key, 2)
    noise = jnp.exp(jax.random.uniform(key, (D,), jnp.float32, math.log(0.5), math.log(2.0)))
    level = 2.0
    return level * row_scale * row_scale * noise


def draw_col_old(key, part):
    row_scale, col_scale = shared_scales(key)
    key = jax.random.fold_in(key, 3)
    noise = jnp.exp(jax.random.uniform(key, (FF,), jnp.float32, math.log(0.5), math.log(2.0)))
    level = 2.0
    return level * col_scale * col_scale * noise


def block_levels(rng, extent, shards, smallest, largest):
    loudness, own = 1.0, jax.random.fold_in(rng, 6)
    for position, blocks in shards:
        draws = jnp.exp(jax.random.uniform(jax.random.fold_in(own, position), (blocks,), jnp.float32, smallest / len(shards), largest / len(shards)))
        loudness = loudness * jnp.repeat(draws, extent[position] // blocks).reshape([-1 if axis == position else 1 for axis in range(len(extent))])
    return loudness


def scatter_about(stream_key, dims, scale, limit, cuts=(), held_as=jnp.bfloat16):
    loudness = block_levels(stream_key, dims, cuts, -0.22, 0.18) if cuts else 1.0
    drawn = jax.random.normal(stream_key, dims, jnp.float32) * scale * loudness
    return jnp.minimum(jnp.maximum(drawn, -limit), limit).astype(held_as)


def setup_inputs(seed: int = 0) -> dict:
    seeds = jax.random.split(jax.random.key(seed), 5)
    return {
        "gradient": draw_gradient(jax.random.fold_in(seeds[4], 71), 0),
        "weights": scatter_about(seeds[1], (D, FF), 0.015, 0.06, ((0, 8), (1, 32)), jnp.float32),
        "row_old": draw_row_old(jax.random.fold_in(seeds[4], 71), 0),
        "col_old": draw_col_old(jax.random.fold_in(seeds[4], 71), 0),
    }


decay_rate = 0.8
tiny_value = 1e-30
clip_limit = 0.1
step_size = 0.25

def reference(gradient, weights, row_old, col_old):
    values = gradient.astype(jnp.float32)
    squares = values * values + tiny_value
    row_moment = decay_rate * row_old + (1.0 - decay_rate) * lax.optimization_barrier(jnp.mean(squares, axis=1))
    col_moment = decay_rate * col_old + (1.0 - decay_rate) * lax.optimization_barrier(jnp.mean(squares, axis=0))
    update = values * lax.rsqrt(row_moment[:, None] * col_moment[None, :])
    spread = jnp.sqrt(jnp.mean(update * update))
    factor = 1.0 / jnp.maximum(1.0, spread / clip_limit)
    return (weights - step_size * factor * update, row_moment, col_moment)
```

```python
import jax
import jax.numpy as jnp
from jax import lax
from jax.experimental import pallas as pl
from jax.experimental.pallas import tpu as pltpu
from jax.sharding import PartitionSpec as P

D = 9216
FF = 36864

decay_rate = 0.8
tiny_value = 1e-30
clip_limit = 0.1
step_size = 0.25

NZ, NX = 8, 4
NC = NZ * NX
NR = 8
SUB = D // NR // NC
MAIN = 32
REST = SUB - MAIN
W = FF // NC
CH = W // 128
PAIR = 2 * SUB
NP = NC // 2
F32 = jnp.float32
MESH = pl.DeviceIdType.MESH


def far_first(i):
    return 4 + (1 - 2 * (i % 2)) * ((i + 1) // 2)


def gather_kernel(
    g_hbm, row_old, col_old,
    u, scale, colm, rowm,
    gv, main, pack1, rest1, pack2, rest2, stage1, stage2, inv_out, inv_in, inv_col,
    sums, acc, total, totals,
    sem_g, main_s, main_r, inv_s, inv_r, r1_s, r1_r, r2_s, r2_r, sum_s, sum_r, tot_s, tot_r,
):
    row = lax.axis_index("row")
    me = lax.axis_index("col")
    z, x = me // NX, me % NX

    def peer(o):
        return lax.rem(z + o // NX, NZ) * NX + lax.rem(x + o % NX, NX)

    load = pltpu.make_async_copy(g_hbm, gv, sem_g)
    load.start()

    barrier = pltpu.get_barrier_semaphore()

    @pl.loop(1, NC)
    def _(o):
        pl.semaphore_signal(barrier, inc=1, device_id={"col": peer(o)}, device_id_type=MESH)

    @pl.loop(1, NR)
    def _(o):
        pl.semaphore_signal(barrier, inc=1, device_id={"row": lax.rem(row + o, NR)}, device_id_type=MESH)

    pl.semaphore_wait(barrier, NC - 1 + NR - 1)

    def block_cols(k):
        return pl.ds(pl.multiple_of(k * W, 128), W)

    def main_copy(k):
        return pltpu.make_async_remote_copy(
            src_ref=g_hbm.at[pl.ds(0, MAIN), block_cols(k)],
            dst_ref=main.at[me],
            send_sem=main_s.at[k],
            recv_sem=main_r.at[me],
            device_id={"col": k},
            device_id_type=MESH,
        )

    def main_wait(k):
        pltpu.make_async_copy(
            g_hbm.at[pl.ds(0, MAIN), pl.ds(0, W)], main.at[k], main_r.at[k]
        ).wait()

    def send_main(i):
        dz = far_first(i)

        @pl.loop(0, NX)
        def _(dx):
            k = lax.rem(z + dz, NZ) * NX + lax.rem(x + dx, NX)

            @pl.when(k != me)
            def _():
                main_copy(k).start()

    pltpu.make_async_copy(
        g_hbm.at[pl.ds(0, MAIN), block_cols(me)], main.at[me], main_r.at[me]
    ).start()

    @pl.loop(0, 3)
    def _(i):
        send_main(i)

    load.wait()

    def rest1_copy(zd):
        return pltpu.make_async_remote_copy(
            src_ref=pack1.at[zd],
            dst_ref=rest1.at[z],
            send_sem=r1_s.at[zd],
            recv_sem=r1_r.at[z],
            device_id={"col": zd * NX + x},
            device_id_type=MESH,
        )

    @pl.loop(0, NZ)
    def _(dz):
        zd = lax.rem(z + dz, NZ)
        for xd in range(NX):
            cols = pl.ds(pl.multiple_of((zd * NX + xd) * W, 128), W)
            stage1[xd * REST : (xd + 1) * REST, :] = gv[MAIN:SUB, cols].astype(F32)
        pack1[zd] = stage1[...].astype(jnp.bfloat16)

        @pl.when(dz != 0)
        def _():
            rest1_copy(zd).start()

        @pl.when(dz == 0)
        def _():
            rest1[zd] = stage1[...].astype(jnp.bfloat16)

    def add_up(k, carry):
        for c in range(CH):
            v = gv[:, pl.ds(pl.multiple_of(k * W + c * 128, 128), 128)].astype(F32)
            carry = carry + v * v
        return carry

    squares = lax.fori_loop(0, NC, add_up, jnp.zeros((SUB, 128), F32))
    sums_row = jnp.sum(squares, axis=1, keepdims=True)
    diagonal = lax.broadcasted_iota(jnp.int32, (SUB, 128), 0) == lax.broadcasted_iota(
        jnp.int32, (SUB, 128), 1
    )
    in_lanes = jnp.sum(
        jnp.where(diagonal, jnp.broadcast_to(sums_row, (SUB, 128)), 0.0), axis=0, keepdims=True
    )
    moment = decay_rate * row_old[...] + (1.0 - decay_rate) * (
        in_lanes[:, :SUB] * (1.0 / FF) + tiny_value
    )
    rowm[...] = moment
    inv_out[...] = jnp.zeros_like(inv_out)
    inv_out[:, :SUB] = lax.rsqrt(moment)
    inv_in[pl.ds(me, 1)] = inv_out[...].reshape(1, 1, 128)

    def inv_copy(k):
        return pltpu.make_async_remote_copy(
            src_ref=inv_out,
            dst_ref=inv_in.at[me],
            send_sem=inv_s.at[k],
            recv_sem=inv_r.at[me],
            device_id={"col": k},
            device_id_type=MESH,
        )

    @pl.loop(1, NC)
    def _(o):
        inv_copy(peer(o)).start()

    @pl.loop(3, NZ)
    def _(i):
        send_main(i)

    def rest2_copy(xd):
        return pltpu.make_async_remote_copy(
            src_ref=pack2.at[xd],
            dst_ref=rest2.at[x],
            send_sem=r2_s.at[xd],
            recv_sem=r2_r.at[x],
            device_id={"col": z * NX + xd},
            device_id_type=MESH,
        )

    @pl.loop(1, NZ)
    def _(o):
        zs = lax.rem(z + o, NZ)
        pltpu.make_async_copy(pack1.at[zs], rest1.at[zs], r1_r.at[zs]).wait()

    for xd in range(NX):
        for zs in range(NZ):
            stage2[xd, zs * REST : (zs + 1) * REST, :] = rest1[zs].astype(F32)[
                xd * REST : (xd + 1) * REST, :
            ]

    @pl.loop(0, NX)
    def _(xd):
        pack2[xd] = stage2[xd].astype(jnp.bfloat16)

        @pl.when(xd != x)
        def _():
            rest2_copy(xd).start()

        @pl.when(xd == x)
        def _():
            rest2[xd] = stage2[xd].astype(jnp.bfloat16)

    @pl.loop(0, NC)
    def _(k):
        @pl.when(k != me)
        def _():
            pltpu.make_async_copy(inv_out, inv_in.at[k], inv_r.at[k]).wait()

        line = inv_in[pl.ds(k, 1)].reshape(1, 128)
        column = jnp.sum(
            jnp.where(diagonal, jnp.broadcast_to(line, (SUB, 128)), 0.0), axis=1, keepdims=True
        )
        inv_col[k] = jnp.broadcast_to(column, (SUB, 128))

    acc[...] = jnp.zeros_like(acc)

    def take(zs):
        for h in range(NX // 2):
            for e in range(2):
                main_wait(zs * NX + 2 * h + e)
            for c in range(CH):
                lanes = slice(c * 128, (c + 1) * 128)
                squares = acc[0, :, lanes]
                scaled = acc[1, :, lanes]
                for e in range(2):
                    k = zs * NX + 2 * h + e
                    v = main[k, :, lanes].astype(F32)
                    w = v * inv_col[k, :MAIN, :]
                    u[zs * 2 + h, e * SUB : e * SUB + MAIN, lanes] = w
                    squares = squares + jnp.sum((v * v).reshape(MAIN // 8, 8, 128), axis=0)
                    scaled = scaled + jnp.sum((w * w).reshape(MAIN // 8, 8, 128), axis=0)
                acc[0, :, lanes] = squares
                acc[1, :, lanes] = scaled

    @pl.loop(0, NZ - 2)
    def _(i):
        take(lax.rem(z + NZ - far_first(i), NZ))

    @pl.loop(0, NX)
    def _(xs):
        @pl.when(xs != x)
        def _():
            pltpu.make_async_copy(pack2.at[xs], rest2.at[xs], r2_r.at[xs]).wait()

    for c in range(CH):
        lanes = slice(c * 128, (c + 1) * 128)
        squares = jnp.zeros((REST, 128), F32)
        scaled = jnp.zeros((REST, 128), F32)
        for xs in range(NX):
            rows = rest2[xs, :, lanes].astype(F32)
            for zs in range(NZ):
                v = rows[zs * REST : (zs + 1) * REST, :]
                w = v * inv_col[zs * NX + xs, MAIN:SUB, :]
                at = (xs % 2) * SUB + MAIN
                u[zs * 2 + xs // 2, at : at + REST, lanes] = w
                squares = squares + v * v
                scaled = scaled + w * w
        acc[0, :REST, lanes] = acc[0, :REST, lanes] + squares
        acc[1, :REST, lanes] = acc[1, :REST, lanes] + scaled

    @pl.loop(NZ - 2, NZ)
    def _(i):
        take(lax.rem(z + NZ - far_first(i), NZ))

    both = jnp.sum(acc[...], axis=1)
    mine = sums.at[row]
    mine[...] = both

    def sum_copy(r):
        return pltpu.make_async_remote_copy(
            src_ref=sums.at[row],
            dst_ref=sums.at[row],
            send_sem=sum_s.at[r],
            recv_sem=sum_r.at[row],
            device_id={"row": r},
            device_id_type=MESH,
        )

    @pl.loop(1, NR)
    def _(o):
        sum_copy(lax.rem(row + o, NR)).start()

    @pl.loop(1, NR)
    def _(o):
        r = lax.rem(row + o, NR)
        pltpu.make_async_copy(sums.at[r], sums.at[r], sum_r.at[r]).wait()

    added = jnp.sum(sums[...], axis=0)
    moments = decay_rate * col_old[...] + (1.0 - decay_rate) * (
        added[0:1, :] * (1.0 / D) + tiny_value
    )
    colm[...] = moments
    inverse = lax.rsqrt(moments)
    part = added[1:2, :] * (inverse * inverse)
    line = part[:, 0:128]
    for c in range(1, CH):
        line = line + part[:, c * 128 : (c + 1) * 128]
    total[...] = line
    totals[pl.ds(me, 1)] = line.reshape(1, 1, 128)

    def total_copy(k):
        return pltpu.make_async_remote_copy(
            src_ref=total,
            dst_ref=totals.at[me],
            send_sem=tot_s.at[k],
            recv_sem=tot_r.at[me],
            device_id={"col": k},
            device_id_type=MESH,
        )

    @pl.loop(1, NC)
    def _(o):
        total_copy(peer(o)).start()

    @pl.loop(1, NC)
    def _(o):
        k = peer(o)
        pltpu.make_async_copy(total, totals.at[k], tot_r.at[k]).wait()

    square_sum = jnp.sum(jnp.sum(totals[...], axis=0), axis=1, keepdims=True)
    factor = 1.0 / jnp.maximum(1.0, jnp.sqrt(square_sum / (D * FF)) / clip_limit)
    scale[...] = (step_size * factor) * inverse

    @pl.loop(1, NC)
    def _(o):
        k = peer(o)
        main_copy(k).wait_send()
        inv_copy(k).wait_send()
        total_copy(k).wait_send()

    @pl.loop(1, NR)
    def _(o):
        sum_copy(lax.rem(row + o, NR)).wait_send()

    @pl.loop(1, NZ)
    def _(o):
        rest1_copy(lax.rem(z + o, NZ)).wait_send()

    @pl.loop(1, NX)
    def _(o):
        rest2_copy(lax.rem(x + o, NX)).wait_send()


def apply_kernel(u, weights, scale, colm_in, rowm_in, out_hbm, colm, rowm, done, sem):
    colm[...] = colm_in[...]
    rowm[...] = rowm_in[...]

    @pl.loop(0, NP)
    def _(p):
        for c in range(CH):
            lanes = slice(c * 128, (c + 1) * 128)
            done[p, :, lanes] = weights[p, :, lanes] - scale[:, lanes] * u[p, :, lanes]
        pltpu.make_async_copy(done.at[p], out_hbm.at[p], sem.at[p]).start()

    @pl.loop(0, NP)
    def _(p):
        pltpu.make_async_copy(done.at[p], out_hbm.at[p], sem.at[p]).wait()


def local(gradient, weights, row_old, col_old):
    vmem = pl.BlockSpec(memory_space=pltpu.VMEM)
    bf16 = jnp.bfloat16
    dma = pltpu.SemaphoreType.DMA
    u, scale, colm, rowm = pl.pallas_call(
        gather_kernel,
        out_shape=(
            pltpu.VMEM((NP, PAIR, W), F32),
            pltpu.VMEM((1, W), F32),
            pltpu.VMEM((1, W), F32),
            pltpu.VMEM((1, SUB), F32),
        ),
        in_specs=[pl.BlockSpec(memory_space=pltpu.HBM), vmem, vmem],
        out_specs=(vmem, vmem, vmem, vmem),
        scratch_shapes=[
            pltpu.VMEM((SUB, FF), bf16),
            pltpu.VMEM((NC, MAIN, W), bf16),
            pltpu.VMEM((NZ, NX * REST, W), bf16),
            pltpu.VMEM((NZ, NX * REST, W), bf16),
            pltpu.VMEM((NX, NZ * REST, W), bf16),
            pltpu.VMEM((NX, NZ * REST, W), bf16),
            pltpu.VMEM((NX * REST, W), F32),
            pltpu.VMEM((NX, NZ * REST, W), F32),
            pltpu.VMEM((1, 128), F32),
            pltpu.VMEM((NC, 1, 128), F32),
            pltpu.VMEM((NC, SUB, 128), F32),
            pltpu.VMEM((NR, 2, W), F32),
            pltpu.VMEM((2, 8, W), F32),
            pltpu.VMEM((1, 128), F32),
            pltpu.VMEM((NC, 1, 128), F32),
            dma, dma((NC,)), dma((NC,)), dma((NC,)), dma((NC,)),
            dma((NZ,)), dma((NZ,)), dma((NX,)), dma((NX,)),
            dma((NR,)), dma((NR,)), dma((NC,)), dma((NC,)),
        ],
        compiler_params=pltpu.CompilerParams(
            collective_id=0, has_side_effects=True, vmem_limit_bytes=24 * 2**20
        ),
        cost_estimate=pl.CostEstimate(
            flops=8 * SUB * FF, bytes_accessed=4 * SUB * FF, transcendentals=0
        ),
        name="gather_kernel",
    )(gradient, row_old.reshape(1, SUB), col_old.reshape(1, W))
    weights = pltpu.with_memory_space_constraint(weights.reshape(NP, PAIR, W), pltpu.VMEM)
    new_weights, colm, rowm = pl.pallas_call(
        apply_kernel,
        out_shape=(
            jax.ShapeDtypeStruct((NP, PAIR, W), F32),
            jax.ShapeDtypeStruct((1, W), F32),
            jax.ShapeDtypeStruct((1, SUB), F32),
        ),
        in_specs=[vmem] * 5,
        out_specs=(pl.BlockSpec(memory_space=pltpu.HBM), vmem, vmem),
        scratch_shapes=[pltpu.VMEM((NP, PAIR, W), F32), dma((NP,))],
        compiler_params=pltpu.CompilerParams(vmem_limit_bytes=16 * 2**20),
        cost_estimate=pl.CostEstimate(
            flops=2 * SUB * FF, bytes_accessed=4 * SUB * FF, transcendentals=0
        ),
        name="apply_kernel",
    )(u, weights, scale, colm, rowm)
    return (new_weights.reshape(SUB * NC, W), rowm.reshape(SUB), colm.reshape(W))


def solution(mesh):
    in_specs = (P(("row", "col"), None), P("row", "col"), P(("row", "col")), P("col"))
    out_specs = (P("row", "col"), P(("row", "col")), P("col"))
    return jax.shard_map(local, mesh=mesh, in_specs=in_specs, out_specs=out_specs, check_vma=False)
```

```python
import jax
import jax.numpy as jnp
from jax import lax
from jax.experimental import pallas as pl
from jax.experimental.pallas import tpu as pltpu
from jax.sharding import PartitionSpec as P

D = 9216
FF = 36864

decay_rate = 0.8
tiny_value = 1e-30
clip_limit = 0.1
step_size = 0.25

NZ, NX = 8, 4
NC = NZ * NX
NR = 8
NL = NR * NX
SUB = D // NR // NC
MAIN = 32
REST = SUB - MAIN
W = FF // NC
CH = W // 128
PAIR = 2 * SUB
NP = NC // 2
STRIDE = 13
BATCHES = (6, 5, 5, 5, 5, 5)
F32 = jnp.float32
BF16 = jnp.bfloat16
MESH = pl.DeviceIdType.MESH


def lane_slices():
    return [(c, slice(c * 128, (c + 1) * 128)) for c in range(CH)]


def gather_kernel(
    g_hbm, w_hbm, row_hbm, col_hbm,
    done, colm, rowm,
    weights, row_old, col_old, gv, main, pack1, rest1, pack2, rest2, stage1, stage2,
    inv_out, inv_in, inv_col, part, parts, zsums, moments, inverse, lines, zlines,
    sem_g, sem_w, sem_old, main_s, main_r, inv_s, inv_r, r1_s, r1_r, r2_s, r2_r, small_s, small_r,
):
    row = lax.axis_index("row")
    me = lax.axis_index("col")
    z, x = me // NX, me % NX
    here = row * NX + x

    def peer(o):
        return lax.rem(z + o // NX, NZ) * NX + lax.rem(x + o % NX, NX)

    def source(o):
        return lax.rem(z + NZ - o // NX, NZ) * NX + lax.rem(x + NX - o % NX, NX)

    def level(o):
        r, xd = lax.rem(row + o // NX, NR), lax.rem(x + o % NX, NX)
        return r * NX + xd, {"row": r, "col": z * NX + xd}

    load = pltpu.make_async_copy(g_hbm, gv, sem_g)
    load.start()
    load_row = pltpu.make_async_copy(row_hbm, row_old, sem_old.at[0])
    load_row.start()
    load_col = pltpu.make_async_copy(col_hbm, col_old, sem_old.at[1])
    load_col.start()
    load_weights = pltpu.make_async_copy(w_hbm, weights, sem_w)

    barrier = pltpu.get_barrier_semaphore()

    @pl.loop(1, NC)
    def _(o):
        pl.semaphore_signal(barrier, inc=1, device_id={"col": peer(o)}, device_id_type=MESH)

    @pl.loop(NX, NL)
    def _(o):
        pl.semaphore_signal(barrier, inc=1, device_id=level(o)[1], device_id_type=MESH)

    pl.semaphore_wait(barrier, NC - 1 + NL - NX)

    def block_cols(k):
        return pl.ds(pl.multiple_of(k * W, 128), W)

    def main_copy(k):
        return pltpu.make_async_remote_copy(
            src_ref=g_hbm.at[pl.ds(0, MAIN), block_cols(k)],
            dst_ref=main.at[me],
            send_sem=main_s.at[k],
            recv_sem=main_r.at[me],
            device_id={"col": k},
            device_id_type=MESH,
        )

    def main_wait(k):
        pltpu.make_async_copy(
            g_hbm.at[pl.ds(0, MAIN), pl.ds(0, W)], main.at[k], main_r.at[k]
        ).wait()

    def send_batch(n):
        first = 1 + sum(BATCHES[:n])

        @pl.loop(first, first + BATCHES[n])
        def _(j):
            main_copy(peer(lax.rem(j * STRIDE, NC))).start()

    def send_level(n, src, dst):
        @pl.loop(1, NL)
        def _(o):
            k, device = level(o)
            pltpu.make_async_remote_copy(
                src_ref=src(k),
                dst_ref=dst,
                send_sem=small_s.at[n],
                recv_sem=small_r.at[n],
                device_id=device,
                device_id_type=MESH,
            ).start()

    def send_z(n, ref):
        @pl.loop(1, NZ)
        def _(o):
            pltpu.make_async_remote_copy(
                src_ref=ref.at[z],
                dst_ref=ref.at[z],
                send_sem=small_s.at[n],
                recv_sem=small_r.at[n],
                device_id={"col": lax.rem(z + o, NZ) * NX + x},
                device_id_type=MESH,
            ).start()

    def wait_small(sem, ref, count):
        some = ref.at[pl.ds(0, count)]
        pltpu.make_async_copy(some, some, sem).wait()

    send_batch(0)

    load.wait()

    def add_up(k, carry):
        for c in range(CH):
            v = gv[:, pl.ds(pl.multiple_of(k * W + c * 128, 128), 128)].astype(F32)
            square = v * v
            part[k, c : c + 1, :] = jnp.sum(square, axis=0, keepdims=True)
            carry = carry + square
        return carry

    squares = lax.fori_loop(0, NC, add_up, jnp.zeros((SUB, 128), F32))

    parts[pl.ds(here, 1)] = part[pl.ds(here, 1)]
    send_level(0, lambda k: part.at[k], parts.at[here])

    sums_row = jnp.sum(squares, axis=1, keepdims=True)
    diagonal = lax.broadcasted_iota(jnp.int32, (SUB, 128), 0) == lax.broadcasted_iota(
        jnp.int32, (SUB, 128), 1
    )
    in_lanes = jnp.sum(
        jnp.where(diagonal, jnp.broadcast_to(sums_row, (SUB, 128)), 0.0), axis=0, keepdims=True
    )
    load_row.wait()
    moment = decay_rate * row_old[...] + (1.0 - decay_rate) * (
        in_lanes[:, :SUB] * (1.0 / FF) + tiny_value
    )
    rowm[...] = moment
    inv_out[...] = jnp.zeros_like(inv_out)
    inv_out[:, :SUB] = lax.rsqrt(moment)
    inv_in[pl.ds(me, 1)] = inv_out[...].reshape(1, 1, 128)

    def inv_copy(k):
        return pltpu.make_async_remote_copy(
            src_ref=inv_out,
            dst_ref=inv_in.at[me],
            send_sem=inv_s.at[k],
            recv_sem=inv_r.at[me],
            device_id={"col": k},
            device_id_type=MESH,
        )

    @pl.loop(1, NC)
    def _(o):
        inv_copy(peer(o)).start()

    def rest1_copy(zd):
        return pltpu.make_async_remote_copy(
            src_ref=pack1.at[zd],
            dst_ref=rest1.at[z],
            send_sem=r1_s.at[zd],
            recv_sem=r1_r.at[z],
            device_id={"col": zd * NX + x},
            device_id_type=MESH,
        )

    @pl.loop(0, NZ)
    def _(dz):
        zd = lax.rem(z + dz, NZ)
        for xd in range(NX):
            cols = pl.ds(pl.multiple_of((zd * NX + xd) * W, 128), W)
            stage1[xd * REST : (xd + 1) * REST, :] = gv[MAIN:SUB, cols].astype(F32)
        pack1[zd] = stage1[...].astype(BF16)

        @pl.when(dz != 0)
        def _():
            rest1_copy(zd).start()

        @pl.when(dz == 0)
        def _():
            rest1[zd] = stage1[...].astype(BF16)

    send_batch(1)
    load_weights.start()
    pltpu.make_async_copy(
        g_hbm.at[pl.ds(0, MAIN), block_cols(me)], main.at[me], main_r.at[me]
    ).start()
    load_col.wait()
    wait_small(small_r.at[0], parts, NL - 1)

    old = decay_rate * col_old[...] + (1.0 - decay_rate) * tiny_value
    old = jnp.where(z == row, old, jnp.zeros_like(old))
    zsums[pl.ds(z, 1)] = (jnp.sum(parts[...], axis=0) * ((1.0 - decay_rate) / D) + old)[None]
    send_z(1, zsums)
    send_batch(2)

    def rest2_copy(xd):
        return pltpu.make_async_remote_copy(
            src_ref=pack2.at[xd],
            dst_ref=rest2.at[x],
            send_sem=r2_s.at[xd],
            recv_sem=r2_r.at[x],
            device_id={"col": z * NX + xd},
            device_id_type=MESH,
        )

    wait_small(small_r.at[1], zsums, NZ - 1)

    moments[pl.ds(here, 1)] = jnp.sum(zsums[...], axis=0)[None]
    send_level(2, lambda k: moments.at[here], moments.at[here])
    send_batch(3)

    @pl.loop(1, NZ)
    def _(o):
        zs = lax.rem(z + o, NZ)
        pltpu.make_async_copy(pack1.at[zs], rest1.at[zs], r1_r.at[zs]).wait()

    for xd in range(NX):
        for zs in range(NZ):
            stage2[xd, zs * REST : (zs + 1) * REST, :] = rest1[zs].astype(F32)[
                xd * REST : (xd + 1) * REST, :
            ]

    wait_small(small_r.at[2], moments, NL - 1)
    colm[...] = moments[pl.ds(me, 1)].reshape(CH, 128)

    @pl.loop(0, NC)
    def _(k):
        inverse[k] = 1.0 / moments[k]

    def add_updates(k, carry):
        for c in range(CH):
            v = gv[:, pl.ds(pl.multiple_of(k * W + c * 128, 128), 128)].astype(F32)
            carry = carry + v * v * inverse[k, c : c + 1, :]
        return carry

    updates = lax.fori_loop(0, NC, add_updates, jnp.zeros((SUB, 128), F32))

    def as_column(line):
        column = jnp.sum(
            jnp.where(diagonal, jnp.broadcast_to(line, (SUB, 128)), 0.0), axis=1, keepdims=True
        )
        return jnp.broadcast_to(column, (SUB, 128))

    mine = as_column(inv_out[...])
    lines[pl.ds(here, 1)] = jnp.sum(updates * (mine * mine), axis=0, keepdims=True)[None]
    send_level(3, lambda k: lines.at[here], lines.at[here])
    send_batch(4)

    @pl.loop(0, NX)
    def _(xd):
        pack2[xd] = stage2[xd].astype(BF16)

        @pl.when(xd != x)
        def _():
            rest2_copy(xd).start()

        @pl.when(xd == x)
        def _():
            rest2[xd] = stage2[xd].astype(BF16)

    wait_small(small_r.at[3], lines, NL - 1)

    zlines[pl.ds(z, 1)] = jnp.sum(lines[...], axis=0)[None]
    send_z(4, zlines)
    send_batch(5)

    @pl.loop(0, NC)
    def _(k):
        @pl.when(k != me)
        def _():
            pltpu.make_async_copy(inv_out, inv_in.at[k], inv_r.at[k]).wait()

        inv_col[k] = as_column(inv_in[pl.ds(k, 1)].reshape(1, 128))

    load_weights.wait()

    @pl.loop(1, NC)
    def _(o):
        inv_copy(peer(o)).wait_send()

    @pl.loop(1, NZ)
    def _(o):
        rest1_copy(lax.rem(z + o, NZ)).wait_send()

    @pl.loop(1, NX)
    def _(o):
        rest2_copy(lax.rem(x + o, NX)).wait_send()

    wait_small(small_s.at[0], parts, NL - 1)
    wait_small(small_s.at[1], zsums, NZ - 1)
    wait_small(small_s.at[2], moments, NL - 1)
    wait_small(small_s.at[3], lines, NL - 1)
    wait_small(small_s.at[4], zlines, NZ - 1)
    wait_small(small_r.at[4], zlines, NZ - 1)

    square_sum = jnp.sum(jnp.sum(zlines[...], axis=0), axis=1, keepdims=True)
    factor = 1.0 / jnp.maximum(1.0, jnp.sqrt(square_sum / (D * FF)) / clip_limit)
    scale = (step_size * factor) * lax.rsqrt(colm[...])

    def finish(j):
        k = source(lax.rem(j * STRIDE, NC))
        main_wait(k)
        p = k // 2
        for e in range(2):

            @pl.when(k % 2 == e)
            def _():
                rows = slice(e * SUB, e * SUB + MAIN)
                for c, lanes in lane_slices():
                    v = main[k, :, lanes].astype(F32) * inv_col[k, :MAIN, :]
                    done[p, rows, lanes] = weights[p, rows, lanes] - scale[c : c + 1, :] * v

    @pl.loop(0, NC - 8)
    def _(j):
        finish(j)

    @pl.loop(0, NX)
    def _(xs):
        @pl.when(xs != x)
        def _():
            pltpu.make_async_copy(pack2.at[xs], rest2.at[xs], r2_r.at[xs]).wait()

    for c, lanes in lane_slices():
        for xs in range(NX):
            values = rest2[xs, :, lanes].astype(F32)
            at = (xs % 2) * SUB + MAIN
            rows = slice(at, at + REST)
            for zs in range(NZ):
                v = values[zs * REST : (zs + 1) * REST, :] * inv_col[zs * NX + xs, MAIN:SUB, :]
                p = zs * 2 + xs // 2
                done[p, rows, lanes] = weights[p, rows, lanes] - scale[c : c + 1, :] * v

    @pl.loop(NC - 8, NC)
    def _(j):
        finish(j)

    @pl.loop(1, NC)
    def _(o):
        main_copy(peer(o)).wait_send()


def write_kernel(done, colm_in, rowm_in, out_hbm, colm, rowm, sem):
    @pl.loop(0, NP)
    def _(p):
        pltpu.make_async_copy(done.at[p], out_hbm.at[p], sem.at[p]).start()

    colm[...] = colm_in[...]
    rowm[...] = rowm_in[...]

    @pl.loop(0, NP)
    def _(p):
        pltpu.make_async_copy(done.at[p], out_hbm.at[p], sem.at[p]).wait()


def local(gradient, weights, row_old, col_old):
    vmem = pl.BlockSpec(memory_space=pltpu.VMEM)
    hbm = pl.BlockSpec(memory_space=pltpu.HBM)
    dma = pltpu.SemaphoreType.DMA
    arrays = (
        gradient, weights.reshape(NP, PAIR, W), row_old.reshape(1, SUB), col_old.reshape(CH, 128)
    )
    done, colm, rowm = pl.pallas_call(
        gather_kernel,
        out_shape=(
            pltpu.VMEM((NP, PAIR, W), F32),
            pltpu.VMEM((CH, 128), F32),
            pltpu.VMEM((1, SUB), F32),
        ),
        in_specs=[hbm] * 4,
        out_specs=(vmem,) * 3,
        scratch_shapes=[
            pltpu.VMEM((NP, PAIR, W), F32),
            pltpu.VMEM((1, SUB), F32),
            pltpu.VMEM((CH, 128), F32),
            pltpu.VMEM((SUB, FF), BF16),
            pltpu.VMEM((NC, MAIN, W), BF16),
            pltpu.VMEM((NZ, NX * REST, W), BF16),
            pltpu.VMEM((NZ, NX * REST, W), BF16),
            pltpu.VMEM((NX, NZ * REST, W), BF16),
            pltpu.VMEM((NX, NZ * REST, W), BF16),
            pltpu.VMEM((NX * REST, W), F32),
            pltpu.VMEM((NX, NZ * REST, W), F32),
            pltpu.VMEM((1, 128), F32),
            pltpu.VMEM((NC, 1, 128), F32),
            pltpu.VMEM((NC, SUB, 128), F32),
            pltpu.VMEM((NC, CH, 128), F32),
            pltpu.VMEM((NL, CH, 128), F32),
            pltpu.VMEM((NZ, CH, 128), F32),
            pltpu.VMEM((NL, CH, 128), F32),
            pltpu.VMEM((NC, CH, 128), F32),
            pltpu.VMEM((NL, 1, 128), F32),
            pltpu.VMEM((NZ, 1, 128), F32),
            dma, dma, dma((2,)), dma((NC,)), dma((NC,)), dma((NC,)), dma((NC,)),
            dma((NZ,)), dma((NZ,)), dma((NX,)), dma((NX,)), dma((5,)), dma((5,)),
        ],
        compiler_params=pltpu.CompilerParams(
            collective_id=0, has_side_effects=True, vmem_limit_bytes=28 * 2**20
        ),
        cost_estimate=pl.CostEstimate(
            flops=8 * SUB * FF, bytes_accessed=4 * SUB * FF, transcendentals=0
        ),
        name="gather_kernel",
    )(*[pltpu.with_memory_space_constraint(a, pltpu.HBM) for a in arrays])
    new_weights, colm, rowm = pl.pallas_call(
        write_kernel,
        out_shape=(
            jax.ShapeDtypeStruct((NP, PAIR, W), F32),
            jax.ShapeDtypeStruct((CH, 128), F32),
            jax.ShapeDtypeStruct((1, SUB), F32),
        ),
        in_specs=[vmem] * 3,
        out_specs=(hbm, vmem, vmem),
        scratch_shapes=[dma((NP,))],
        compiler_params=pltpu.CompilerParams(vmem_limit_bytes=2**20),
        cost_estimate=pl.CostEstimate(
            flops=2 * SUB * FF, bytes_accessed=4 * SUB * FF, transcendentals=0
        ),
        name="write_kernel",
    )(done, colm, rowm)
    return (new_weights.reshape(SUB * NC, W), rowm.reshape(SUB), colm.reshape(W))


def solution(mesh):
    in_specs = (P(("row", "col"), None), P("row", "col"), P(("row", "col")), P("col"))
    out_specs = (P("row", "col"), P(("row", "col")), P("col"))
    return jax.shard_map(local, mesh=mesh, in_specs=in_specs, out_specs=out_specs, check_vma=False)
```

```python
import jax
import jax.numpy as jnp
from jax import lax
from jax.experimental import pallas as pl
from jax.experimental.pallas import tpu as pltpu
from jax.sharding import PartitionSpec as P

D = 9216
FF = 36864

decay_rate = 0.8
tiny_value = 1e-30
clip_limit = 0.1
step_size = 0.25

NZ, NX = 8, 4
NC = NZ * NX
NR = 8
NL = NR * NX
SUB = D // NR // NC
MAIN = 32
REST = SUB - MAIN
W = FF // NC
CH = W // 128
PAIR = 2 * SUB
NP = NC // 2
ORDER = (0,13, 26, 7, 20, 14, 27, 8, 21, 15, 28, 9, 22, 16, 29, 10, 23, 4, 17, 30, 11, 24, 5, 18, 31, 12, 25, 6, 19, 1, 2, 3)
BATCHES = (6, 6, 6, 5, 4, 4)
F32 = jnp.float32
BF16 = jnp.bfloat16
MESH = pl.DeviceIdType.MESH


def lane_slices():
    return [(c, slice(c * 128, (c + 1) * 128)) for c in range(CH)]


def gather_kernel(
    g_hbm, w_hbm, row_hbm, col_hbm,
    done, colm, rowm,
    weights, row_old, col_old, gv, main, pack1, rest1, pack2, rest2, stage1, stage2,
    inv_out, inv_in, inv_col, part, parts, zsums, moments, inverse, lines, zlines,
    sem_g, sem_w, sem_old, main_s, main_r, inv_s, inv_r, r1_s, r1_r, r2_s, r2_r, small_s, small_r,
):
    row = lax.axis_index("row")
    me = lax.axis_index("col")
    z, x = me // NX, me % NX
    here = row * NX + x

    def peer(o):
        return lax.rem(z + o // NX, NZ) * NX + lax.rem(x + o % NX, NX)

    def source(o):
        return lax.rem(z + NZ - o // NX, NZ) * NX + lax.rem(x + NX - o % NX, NX)

    def offset(j):
        o = 0
        for i in range(1, NC):
            o = jnp.where(j == i, ORDER[i], o)
        return o

    def level(o):
        r, xd = lax.rem(row + o // NX, NR), lax.rem(x + o % NX, NX)
        return r * NX + xd, {"row": r, "col": z * NX + xd}

    barrier = pltpu.get_barrier_semaphore()
    z_at = [lax.rem(z + d, NZ) * NX for d in range(NZ)]
    x_at = [lax.rem(x + d, NX) for d in range(NX)]
    r_at = [lax.rem(row + d, NR) for d in range(NR)]

    def far(d, n):
        return min(d, n - d)

    near = [(0, dz, dx) for dz in range(NZ) for dx in range(NX) if dz or dx]
    near += [(dr, 0, dx) for dr in range(1, NR) for dx in range(NX)]
    near.sort(key=lambda o: -far(o[0], NR) // 2 - far(o[1], NZ) - far(o[2], NX))
    for dr, dz, dx in near:
        pl.semaphore_signal(
            barrier,
            inc=1,
            device_id={"row": r_at[dr], "col": z_at[dz] + x_at[dx]},
            device_id_type=MESH,
        )

    load = pltpu.make_async_copy(g_hbm, gv, sem_g)
    load.start()
    load_row = pltpu.make_async_copy(row_hbm, row_old, sem_old.at[0])
    load_row.start()
    load_col = pltpu.make_async_copy(col_hbm, col_old, sem_old.at[1])
    load_col.start()
    load_weights = pltpu.make_async_copy(w_hbm, weights, sem_w)

    pl.semaphore_wait(barrier, NC - 1 + NL - NX)

    def block_cols(k):
        return pl.ds(pl.multiple_of(k * W, 128), W)

    def main_copy(k):
        return pltpu.make_async_remote_copy(
            src_ref=g_hbm.at[pl.ds(0, MAIN), block_cols(k)],
            dst_ref=main.at[me],
            send_sem=main_s.at[k],
            recv_sem=main_r.at[me],
            device_id={"col": k},
            device_id_type=MESH,
        )

    def main_wait(k):
        pltpu.make_async_copy(
            g_hbm.at[pl.ds(0, MAIN), pl.ds(0, W)], main.at[k], main_r.at[k]
        ).wait()

    def send_batch(n):
        first = 1 + sum(BATCHES[:n])

        @pl.loop(first, first + BATCHES[n])
        def _(j):
            main_copy(peer(offset(j))).start()

    def send_level(n, src, dst):
        @pl.loop(1, NL)
        def _(o):
            k, device = level(o)
            pltpu.make_async_remote_copy(
                src_ref=src(k),
                dst_ref=dst,
                send_sem=small_s.at[n],
                recv_sem=small_r.at[n],
                device_id=device,
                device_id_type=MESH,
            ).start()

    def send_z(n, ref):
        @pl.loop(1, NZ)
        def _(o):
            pltpu.make_async_remote_copy(
                src_ref=ref.at[z],
                dst_ref=ref.at[z],
                send_sem=small_s.at[n],
                recv_sem=small_r.at[n],
                device_id={"col": lax.rem(z + o, NZ) * NX + x},
                device_id_type=MESH,
            ).start()

    def wait_small(sem, ref, count):
        some = ref.at[pl.ds(0, count)]
        pltpu.make_async_copy(some, some, sem).wait()

    send_batch(0)

    load.wait()

    def add_up(k, carry):
        for c in range(CH):
            v = gv[:, pl.ds(pl.multiple_of(k * W + c * 128, 128), 128)].astype(F32)
            square = v * v
            part[k, c : c + 1, :] = jnp.sum(square, axis=0, keepdims=True)
            carry = carry + square
        return carry

    squares = lax.fori_loop(0, NC, add_up, jnp.zeros((SUB, 128), F32))

    parts[pl.ds(here, 1)] = part[pl.ds(here, 1)]
    send_level(0, lambda k: part.at[k], parts.at[here])

    sums_row = jnp.sum(squares, axis=1, keepdims=True)
    diagonal = lax.broadcasted_iota(jnp.int32, (SUB, 128), 0) == lax.broadcasted_iota(
        jnp.int32, (SUB, 128), 1
    )
    in_lanes = jnp.sum(
        jnp.where(diagonal, jnp.broadcast_to(sums_row, (SUB, 128)), 0.0), axis=0, keepdims=True
    )
    load_row.wait()
    moment = decay_rate * row_old[...] + (1.0 - decay_rate) * (
        in_lanes[:, :SUB] * (1.0 / FF) + tiny_value
    )
    rowm[...] = moment
    inv_out[...] = jnp.zeros_like(inv_out)
    inv_out[:, :SUB] = lax.rsqrt(moment)
    inv_in[pl.ds(me, 1)] = inv_out[...].reshape(1, 1, 128)

    def inv_copy(k):
        return pltpu.make_async_remote_copy(
            src_ref=inv_out,
            dst_ref=inv_in.at[me],
            send_sem=inv_s.at[k],
            recv_sem=inv_r.at[me],
            device_id={"col": k},
            device_id_type=MESH,
        )

    @pl.loop(1, NC)
    def _(o):
        inv_copy(peer(o)).start()

    def rest1_copy(zd):
        return pltpu.make_async_remote_copy(
            src_ref=pack1.at[zd],
            dst_ref=rest1.at[z],
            send_sem=r1_s.at[zd],
            recv_sem=r1_r.at[z],
            device_id={"col": zd * NX + x},
            device_id_type=MESH,
        )

    @pl.loop(0, NZ)
    def _(dz):
        zd = lax.rem(z + dz, NZ)
        for xd in range(NX):
            cols = pl.ds(pl.multiple_of((zd * NX + xd) * W, 128), W)
            stage1[xd * REST : (xd + 1) * REST, :] = gv[MAIN:SUB, cols].astype(F32)
        pack1[zd] = stage1[...].astype(BF16)

        @pl.when(dz != 0)
        def _():
            rest1_copy(zd).start()

        @pl.when(dz == 0)
        def _():
            rest1[zd] = stage1[...].astype(BF16)

    send_batch(1)
    load_weights.start()
    pltpu.make_async_copy(
        g_hbm.at[pl.ds(0, MAIN), block_cols(me)], main.at[me], main_r.at[me]
    ).start()
    load_col.wait()
    wait_small(small_r.at[0], parts, NL - 1)

    old = decay_rate * col_old[...] + (1.0 - decay_rate) * tiny_value
    old = jnp.where(z == row, old, jnp.zeros_like(old))
    zsums[pl.ds(z, 1)] = (jnp.sum(parts[...], axis=0) * ((1.0 - decay_rate) / D) + old)[None]
    send_z(1, zsums)
    send_batch(2)

    def rest2_copy(xd):
        return pltpu.make_async_remote_copy(
            src_ref=pack2.at[xd],
            dst_ref=rest2.at[x],
            send_sem=r2_s.at[xd],
            recv_sem=r2_r.at[x],
            device_id={"col": z * NX + xd},
            device_id_type=MESH,
        )

    wait_small(small_r.at[1], zsums, NZ - 1)

    moments[pl.ds(here, 1)] = jnp.sum(zsums[...], axis=0)[None]
    send_level(2, lambda k: moments.at[here], moments.at[here])
    send_batch(3)

    @pl.loop(1, NZ)
    def _(o):
        zs = lax.rem(z + o, NZ)
        pltpu.make_async_copy(pack1.at[zs], rest1.at[zs], r1_r.at[zs]).wait()

    for xd in range(NX):
        for zs in range(NZ):
            stage2[xd, zs * REST : (zs + 1) * REST, :] = rest1[zs].astype(F32)[
                xd * REST : (xd + 1) * REST, :
            ]

    @pl.loop(0, NX)
    def _(xd):
        pack2[xd] = stage2[xd].astype(BF16)

        @pl.when(xd != x)
        def _():
            rest2_copy(xd).start()

        @pl.when(xd == x)
        def _():
            rest2[xd] = stage2[xd].astype(BF16)

    wait_small(small_r.at[2], moments, NL - 1)
    colm[...] = moments[pl.ds(me, 1)].reshape(CH, 128)

    @pl.loop(0, NC)
    def _(k):
        inverse[k] = 1.0 / moments[k]

    def add_updates(k, carry):
        for c in range(CH):
            v = gv[:, pl.ds(pl.multiple_of(k * W + c * 128, 128), 128)].astype(F32)
            carry = carry + v * v * inverse[k, c : c + 1, :]
        return carry

    updates = lax.fori_loop(0, NC, add_updates, jnp.zeros((SUB, 128), F32))

    def as_column(line):
        column = jnp.sum(
            jnp.where(diagonal, jnp.broadcast_to(line, (SUB, 128)), 0.0), axis=1, keepdims=True
        )
        return jnp.broadcast_to(column, (SUB, 128))

    mine = as_column(inv_out[...])
    lines[pl.ds(here, 1)] = jnp.sum(updates * (mine * mine), axis=0, keepdims=True)[None]
    send_level(3, lambda k: lines.at[here], lines.at[here])
    send_batch(4)

    wait_small(small_r.at[3], lines, NL - 1)

    zlines[pl.ds(z, 1)] = jnp.sum(lines[...], axis=0)[None]
    send_z(4, zlines)
    send_batch(5)

    @pl.loop(0, NC)
    def _(k):
        @pl.when(k != me)
        def _():
            pltpu.make_async_copy(inv_out, inv_in.at[k], inv_r.at[k]).wait()

        inv_col[k] = as_column(inv_in[pl.ds(k, 1)].reshape(1, 128))

    load_weights.wait()

    @pl.loop(1, NC)
    def _(o):
        inv_copy(peer(o)).wait_send()

    @pl.loop(1, NZ)
    def _(o):
        rest1_copy(lax.rem(z + o, NZ)).wait_send()

    @pl.loop(1, NX)
    def _(o):
        rest2_copy(lax.rem(x + o, NX)).wait_send()

    wait_small(small_s.at[0], parts, NL - 1)
    wait_small(small_s.at[1], zsums, NZ - 1)
    wait_small(small_s.at[2], moments, NL - 1)
    wait_small(small_s.at[3], lines, NL - 1)
    wait_small(small_s.at[4], zlines, NZ - 1)
    wait_small(small_r.at[4], zlines, NZ - 1)

    square_sum = jnp.sum(jnp.sum(zlines[...], axis=0), axis=1, keepdims=True)
    factor = 1.0 / jnp.maximum(1.0, jnp.sqrt(square_sum / (D * FF)) / clip_limit)
    scale = (step_size * factor) * lax.rsqrt(colm[...])

    def finish(j):
        at = offset(j)
        k = source(at)

        @pl.when(j > 0)
        def _():
            main_copy(peer(at)).wait_send()

        main_wait(k)
        p = k // 2
        for e in range(2):

            @pl.when(k % 2 == e)
            def _():
                rows = slice(e * SUB, e * SUB + MAIN)
                for c, lanes in lane_slices():
                    v = main[k, :, lanes].astype(F32) * inv_col[k, :MAIN, :]
                    done[p, rows, lanes] = weights[p, rows, lanes] - scale[c : c + 1, :] * v

    @pl.loop(0, NC - 8)
    def _(j):
        finish(j)

    @pl.loop(0, NX)
    def _(xs):
        @pl.when(xs != x)
        def _():
            pltpu.make_async_copy(pack2.at[xs], rest2.at[xs], r2_r.at[xs]).wait()

    for c, lanes in lane_slices():
        for xs in range(NX):
            values = rest2[xs, :, lanes].astype(F32)
            at = (xs % 2) * SUB + MAIN
            rows = slice(at, at + REST)
            for zs in range(NZ):
                v = values[zs * REST : (zs + 1) * REST, :] * inv_col[zs * NX + xs, MAIN:SUB, :]
                p = zs * 2 + xs // 2
                done[p, rows, lanes] = weights[p, rows, lanes] - scale[c : c + 1, :] * v

    @pl.loop(NC - 8, NC)
    def _(j):
        finish(j)


def write_kernel(done, colm, rowm, done_hbm, colm_hbm, rowm_hbm, sem):
    copies = [
        pltpu.make_async_copy(done, done_hbm, sem.at[0]),
        pltpu.make_async_copy(colm, colm_hbm, sem.at[1]),
        pltpu.make_async_copy(rowm, rowm_hbm, sem.at[2]),
    ]
    for copy in copies:
        copy.start()
    for copy in copies:
        copy.wait()


def local(gradient, weights, row_old, col_old):
    vmem = pl.BlockSpec(memory_space=pltpu.VMEM)
    hbm = pl.BlockSpec(memory_space=pltpu.HBM)
    dma = pltpu.SemaphoreType.DMA
    arrays = (
        gradient, weights.reshape(NP, PAIR, W), row_old.reshape(1, SUB), col_old.reshape(CH, 128)
    )
    done, colm, rowm = pl.pallas_call(
        gather_kernel,
        out_shape=(
            pltpu.VMEM((NP, PAIR, W), F32),
            pltpu.VMEM((CH, 128), F32),
            pltpu.VMEM((1, SUB), F32),
        ),
        in_specs=[hbm] * 4,
        out_specs=(vmem,) * 3,
        scratch_shapes=[
            pltpu.VMEM((NP, PAIR, W), F32),
            pltpu.VMEM((1, SUB), F32),
            pltpu.VMEM((CH, 128), F32),
            pltpu.VMEM((SUB, FF), BF16),
            pltpu.VMEM((NC, MAIN, W), BF16),
            pltpu.VMEM((NZ, NX * REST, W), BF16),
            pltpu.VMEM((NZ, NX * REST, W), BF16),
            pltpu.VMEM((NX, NZ * REST, W), BF16),
            pltpu.VMEM((NX, NZ * REST, W), BF16),
            pltpu.VMEM((NX * REST, W), F32),
            pltpu.VMEM((NX, NZ * REST, W), F32),
            pltpu.VMEM((1, 128), F32),
            pltpu.VMEM((NC, 1, 128), F32),
            pltpu.VMEM((NC, SUB, 128), F32),
            pltpu.VMEM((NC, CH, 128), F32),
            pltpu.VMEM((NL, CH, 128), F32),
            pltpu.VMEM((NZ, CH, 128), F32),
            pltpu.VMEM((NL, CH, 128), F32),
            pltpu.VMEM((NC, CH, 128), F32),
            pltpu.VMEM((NL, 1, 128), F32),
            pltpu.VMEM((NZ, 1, 128), F32),
            dma, dma, dma((2,)), dma((NC,)), dma((NC,)), dma((NC,)), dma((NC,)),
            dma((NZ,)), dma((NZ,)), dma((NX,)), dma((NX,)), dma((5,)), dma((5,)),
        ],
        compiler_params=pltpu.CompilerParams(
            collective_id=0, has_side_effects=True, vmem_limit_bytes=28 * 2**20
        ),
        cost_estimate=pl.CostEstimate(
            flops=8 * SUB * FF, bytes_accessed=4 * SUB * FF, transcendentals=0
        ),
        name="gather_kernel",
    )(*[pltpu.with_memory_space_constraint(a, pltpu.HBM) for a in arrays])
    new_weights, colm, rowm = pl.pallas_call(
        write_kernel,
        out_shape=(
            jax.ShapeDtypeStruct((NP, PAIR, W), F32),
            jax.ShapeDtypeStruct((CH, 128), F32),
            jax.ShapeDtypeStruct((1, SUB), F32),
        ),
        in_specs=[vmem] * 3,
        out_specs=(hbm,) * 3,
        scratch_shapes=[dma((3,))],
        compiler_params=pltpu.CompilerParams(vmem_limit_bytes=2**20),
        cost_estimate=pl.CostEstimate(
            flops=2 * SUB * FF, bytes_accessed=4 * SUB * FF, transcendentals=0
        ),
        name="write_kernel",
    )(done, colm, rowm)
    return (new_weights.reshape(SUB * NC, W), rowm.reshape(SUB), colm.reshape(W))


def solution(mesh):
    in_specs = (P(("row", "col"), None), P("row", "col"), P(("row", "col")), P("col"))
    out_specs = (P("row", "col"), P(("row", "col")), P("col"))
    return jax.shard_map(local, mesh=mesh, in_specs=in_specs, out_specs=out_specs, check_vma=False)
```

```python
import jax
import jax.numpy as jnp
from jax import lax
from jax.experimental import pallas as pl
from jax.experimental.pallas import tpu as pltpu
from jax.sharding import PartitionSpec as P

D = 9216
FF = 36864

decay_rate = 0.8
tiny_value = 1e-30
clip_limit = 0.1
step_size = 0.25

NZ, NX = 8, 4
NC = NZ * NX
NR = 8
NL = NR * NX
SUB = D // NR // NC
MAIN = 32
REST = SUB - MAIN
W = FF // NC
CH = W // 128
PAIR = 2 * SUB
NP = NC // 2
ORDER = (0,13, 26, 7, 20, 14, 27, 8, 21, 15, 28, 9, 22, 16, 29, 10, 23, 4, 17, 30, 11, 24, 5, 18, 31, 12, 25, 6, 19, 1, 2, 3)
BATCHES = (6, 6, 6, 5, 4, 4)
F32 = jnp.float32
BF16 = jnp.bfloat16
MESH = pl.DeviceIdType.MESH


def lane_slices():
    return [(c, slice(c * 128, (c + 1) * 128)) for c in range(CH)]


def gather_kernel(
    g_hbm, w_hbm, row_hbm, col_hbm,
    done, colm, rowm,
    weights, row_old, col_old, gv, main, pack1, rest1, pack2, rest2, stage1, stage2,
    inv_out, inv_in, inv_col, part, parts, zsums, moments, inverse, lines, zlines,
    sem_g, sem_w, sem_old, main_s, main_r, inv_s, inv_r, r1_s, r1_r, r2_s, r2_r, small_s, small_r,
):
    row = lax.axis_index("row")
    me = lax.axis_index("col")
    z, x = me // NX, me % NX
    here = row * NX + x

    def peer(o):
        return lax.rem(z + o // NX, NZ) * NX + lax.rem(x + o % NX, NX)

    def source(o):
        return lax.rem(z + NZ - o // NX, NZ) * NX + lax.rem(x + NX - o % NX, NX)

    def offset(j):
        o = 0
        for i in range(1, NC):
            o = jnp.where(j == i, ORDER[i], o)
        return o

    def level(o):
        r, xd = lax.rem(row + o // NX, NR), lax.rem(x + o % NX, NX)
        return r * NX + xd, {"row": r, "col": z * NX + xd}

    barrier = pltpu.get_barrier_semaphore()
    z_at = [lax.rem(z + d, NZ) * NX for d in range(NZ)]
    x_at = [lax.rem(x + d, NX) for d in range(NX)]
    r_at = [lax.rem(row + d, NR) for d in range(NR)]

    def far(d, n):
        return min(d, n - d)

    near = [(0, dz, dx) for dz in range(NZ) for dx in range(NX) if dz or dx]
    near += [(dr, 0, dx) for dr in range(1, NR) for dx in range(NX)]
    near.sort(key=lambda o: -far(o[0], NR) // 2 - far(o[1], NZ) - far(o[2], NX))
    for dr, dz, dx in near:
        pl.semaphore_signal(
            barrier,
            inc=1,
            device_id={"row": r_at[dr], "col": z_at[dz] + x_at[dx]},
            device_id_type=MESH,
        )

    load = pltpu.make_async_copy(g_hbm, gv, sem_g)
    load.start()
    load_row = pltpu.make_async_copy(row_hbm, row_old, sem_old.at[0])
    load_row.start()
    load_col = pltpu.make_async_copy(col_hbm, col_old, sem_old.at[1])
    load_col.start()
    load_weights = pltpu.make_async_copy(w_hbm, weights, sem_w)

    pl.semaphore_wait(barrier, NC - 1 + NL - NX)

    def block_cols(k):
        return pl.ds(pl.multiple_of(k * W, 128), W)

    def main_copy(k):
        return pltpu.make_async_remote_copy(
            src_ref=g_hbm.at[pl.ds(0, MAIN), block_cols(k)],
            dst_ref=main.at[me],
            send_sem=main_s.at[k],
            recv_sem=main_r.at[me],
            device_id={"col": k},
            device_id_type=MESH,
        )

    def main_wait(k):
        pltpu.make_async_copy(
            g_hbm.at[pl.ds(0, MAIN), pl.ds(0, W)], main.at[k], main_r.at[k]
        ).wait()

    def send_batch(n):
        first = 1 + sum(BATCHES[:n])

        @pl.loop(first, first + BATCHES[n])
        def _(j):
            main_copy(peer(offset(j))).start()

    def send_level(n, src, dst):
        @pl.loop(1, NL)
        def _(o):
            k, device = level(o)
            pltpu.make_async_remote_copy(
                src_ref=src(k),
                dst_ref=dst,
                send_sem=small_s.at[n],
                recv_sem=small_r.at[n],
                device_id=device,
                device_id_type=MESH,
            ).start()

    def send_z(n, ref):
        @pl.loop(1, NZ)
        def _(o):
            pltpu.make_async_remote_copy(
                src_ref=ref.at[z],
                dst_ref=ref.at[z],
                send_sem=small_s.at[n],
                recv_sem=small_r.at[n],
                device_id={"col": lax.rem(z + o, NZ) * NX + x},
                device_id_type=MESH,
            ).start()

    def wait_small(sem, ref, count):
        some = ref.at[pl.ds(0, count)]
        pltpu.make_async_copy(some, some, sem).wait()

    send_batch(0)

    load.wait()

    def add_up(k, carry):
        for c in range(CH):
            v = gv[:, pl.ds(pl.multiple_of(k * W + c * 128, 128), 128)].astype(F32)
            square = v * v
            part[k, c : c + 1, :] = jnp.sum(square, axis=0, keepdims=True)
            carry = carry + square
        return carry

    squares = lax.fori_loop(0, NC, add_up, jnp.zeros((SUB, 128), F32))

    parts[pl.ds(here, 1)] = part[pl.ds(here, 1)]
    send_level(0, lambda k: part.at[k], parts.at[here])

    sums_row = jnp.sum(squares, axis=1, keepdims=True)
    diagonal = lax.broadcasted_iota(jnp.int32, (SUB, 128), 0) == lax.broadcasted_iota(
        jnp.int32, (SUB, 128), 1
    )
    in_lanes = jnp.sum(
        jnp.where(diagonal, jnp.broadcast_to(sums_row, (SUB, 128)), 0.0), axis=0, keepdims=True
    )
    load_row.wait()
    moment = decay_rate * row_old[...] + (1.0 - decay_rate) * (
        in_lanes[:, :SUB] * (1.0 / FF) + tiny_value
    )
    rowm[...] = moment
    inv_out[...] = jnp.zeros_like(inv_out)
    inv_out[:, :SUB] = lax.rsqrt(moment)
    inv_in[pl.ds(me, 1)] = inv_out[...].reshape(1, 1, 128)

    def inv_copy(k):
        return pltpu.make_async_remote_copy(
            src_ref=inv_out,
            dst_ref=inv_in.at[me],
            send_sem=inv_s.at[k],
            recv_sem=inv_r.at[me],
            device_id={"col": k},
            device_id_type=MESH,
        )

    def rest1_copy(zd):
        return pltpu.make_async_remote_copy(
            src_ref=pack1.at[zd],
            dst_ref=rest1.at[z],
            send_sem=r1_s.at[zd],
            recv_sem=r1_r.at[z],
            device_id={"col": zd * NX + x},
            device_id_type=MESH,
        )

    @pl.loop(0, NZ)
    def _(dz):
        zd = lax.rem(z + dz, NZ)
        for xd in range(NX):
            cols = pl.ds(pl.multiple_of((zd * NX + xd) * W, 128), W)
            stage1[xd * REST : (xd + 1) * REST, :] = gv[MAIN:SUB, cols].astype(F32)
        pack1[zd] = stage1[...].astype(BF16)

        @pl.when(dz != 0)
        def _():
            rest1_copy(zd).start()

        @pl.when(dz == 0)
        def _():
            rest1[zd] = stage1[...].astype(BF16)

    send_batch(1)
    load_weights.start()
    pltpu.make_async_copy(
        g_hbm.at[pl.ds(0, MAIN), block_cols(me)], main.at[me], main_r.at[me]
    ).start()
    load_col.wait()
    wait_small(small_r.at[0], parts, NL - 1)

    old = decay_rate * col_old[...] + (1.0 - decay_rate) * tiny_value
    old = jnp.where(z == row, old, jnp.zeros_like(old))
    zsums[pl.ds(z, 1)] = (jnp.sum(parts[...], axis=0) * ((1.0 - decay_rate) / D) + old)[None]
    send_z(1, zsums)
    send_batch(2)

    @pl.loop(1, NC)
    def _(o):
        inv_copy(peer(o)).start()


    def rest2_copy(xd):
        return pltpu.make_async_remote_copy(
            src_ref=pack2.at[xd],
            dst_ref=rest2.at[x],
            send_sem=r2_s.at[xd],
            recv_sem=r2_r.at[x],
            device_id={"col": z * NX + xd},
            device_id_type=MESH,
        )

    wait_small(small_r.at[1], zsums, NZ - 1)

    moments[pl.ds(here, 1)] = jnp.sum(zsums[...], axis=0)[None]
    send_level(2, lambda k: moments.at[here], moments.at[here])
    send_batch(3)

    @pl.loop(1, NZ)
    def _(o):
        zs = lax.rem(z + o, NZ)
        pltpu.make_async_copy(pack1.at[zs], rest1.at[zs], r1_r.at[zs]).wait()

    for xd in range(NX):
        for zs in range(NZ):
            stage2[xd, zs * REST : (zs + 1) * REST, :] = rest1[zs].astype(F32)[
                xd * REST : (xd + 1) * REST, :
            ]

    @pl.loop(0, NX)
    def _(xd):
        pack2[xd] = stage2[xd].astype(BF16)

        @pl.when(xd != x)
        def _():
            rest2_copy(xd).start()

        @pl.when(xd == x)
        def _():
            rest2[xd] = stage2[xd].astype(BF16)

    wait_small(small_r.at[2], moments, NL - 1)
    colm[...] = moments[pl.ds(me, 1)].reshape(CH, 128)

    @pl.loop(0, NC)
    def _(k):
        inverse[k] = 1.0 / moments[k]

    def add_updates(k, carry):
        for c in range(CH):
            v = gv[:, pl.ds(pl.multiple_of(k * W + c * 128, 128), 128)].astype(F32)
            carry = carry + v * v * inverse[k, c : c + 1, :]
        return carry

    updates = lax.fori_loop(0, NC, add_updates, jnp.zeros((SUB, 128), F32))

    def as_column(line):
        column = jnp.sum(
            jnp.where(diagonal, jnp.broadcast_to(line, (SUB, 128)), 0.0), axis=1, keepdims=True
        )
        return jnp.broadcast_to(column, (SUB, 128))

    mine = as_column(inv_out[...])
    lines[pl.ds(here, 1)] = jnp.sum(updates * (mine * mine), axis=0, keepdims=True)[None]
    send_level(3, lambda k: lines.at[here], lines.at[here])
    send_batch(4)

    wait_small(small_r.at[3], lines, NL - 1)

    zlines[pl.ds(z, 1)] = jnp.sum(lines[...], axis=0)[None]
    send_z(4, zlines)
    send_batch(5)

    @pl.loop(0, NC)
    def _(k):
        @pl.when(k != me)
        def _():
            pltpu.make_async_copy(inv_out, inv_in.at[k], inv_r.at[k]).wait()

        inv_col[k] = as_column(inv_in[pl.ds(k, 1)].reshape(1, 128))

    load_weights.wait()

    @pl.loop(1, NC)
    def _(o):
        inv_copy(peer(o)).wait_send()

    @pl.loop(1, NZ)
    def _(o):
        rest1_copy(lax.rem(z + o, NZ)).wait_send()

    @pl.loop(1, NX)
    def _(o):
        rest2_copy(lax.rem(x + o, NX)).wait_send()

    wait_small(small_s.at[0], parts, NL - 1)
    wait_small(small_s.at[1], zsums, NZ - 1)
    wait_small(small_s.at[2], moments, NL - 1)
    wait_small(small_s.at[3], lines, NL - 1)
    wait_small(small_s.at[4], zlines, NZ - 1)
    wait_small(small_r.at[4], zlines, NZ - 1)

    square_sum = jnp.sum(jnp.sum(zlines[...], axis=0), axis=1, keepdims=True)
    factor = 1.0 / jnp.maximum(1.0, jnp.sqrt(square_sum / (D * FF)) / clip_limit)
    scale = (step_size * factor) * lax.rsqrt(colm[...])

    def finish(j):
        at = offset(j)
        k = source(at)

        @pl.when(j > 0)
        def _():
            main_copy(peer(at)).wait_send()

        main_wait(k)
        p = k // 2
        for e in range(2):

            @pl.when(k % 2 == e)
            def _():
                rows = slice(e * SUB, e * SUB + MAIN)
                for c, lanes in lane_slices():
                    v = main[k, :, lanes].astype(F32) * inv_col[k, :MAIN, :]
                    done[p, rows, lanes] = weights[p, rows, lanes] - scale[c : c + 1, :] * v

    @pl.loop(0, NC - 8)
    def _(j):
        finish(j)

    @pl.loop(0, NX)
    def _(xs):
        @pl.when(xs != x)
        def _():
            pltpu.make_async_copy(pack2.at[xs], rest2.at[xs], r2_r.at[xs]).wait()

    for c, lanes in lane_slices():
        for xs in range(NX):
            values = rest2[xs, :, lanes].astype(F32)
            at = (xs % 2) * SUB + MAIN
            rows = slice(at, at + REST)
            for zs in range(NZ):
                v = values[zs * REST : (zs + 1) * REST, :] * inv_col[zs * NX + xs, MAIN:SUB, :]
                p = zs * 2 + xs // 2
                done[p, rows, lanes] = weights[p, rows, lanes] - scale[c : c + 1, :] * v

    @pl.loop(NC - 8, NC)
    def _(j):
        finish(j)


def write_kernel(done, colm, rowm, done_hbm, colm_hbm, rowm_hbm, sem):
    copies = [
        pltpu.make_async_copy(done, done_hbm, sem.at[0]),
        pltpu.make_async_copy(colm, colm_hbm, sem.at[1]),
        pltpu.make_async_copy(rowm, rowm_hbm, sem.at[2]),
    ]
    for copy in copies:
        copy.start()
    for copy in copies:
        copy.wait()


def local(gradient, weights, row_old, col_old):
    vmem = pl.BlockSpec(memory_space=pltpu.VMEM)
    hbm = pl.BlockSpec(memory_space=pltpu.HBM)
    dma = pltpu.SemaphoreType.DMA
    arrays = (
        gradient, weights.reshape(NP, PAIR, W), row_old.reshape(1, SUB), col_old.reshape(CH, 128)
    )
    done, colm, rowm = pl.pallas_call(
        gather_kernel,
        out_shape=(
            pltpu.VMEM((NP, PAIR, W), F32),
            pltpu.VMEM((CH, 128), F32),
            pltpu.VMEM((1, SUB), F32),
        ),
        in_specs=[hbm] * 4,
        out_specs=(vmem,) * 3,
        scratch_shapes=[
            pltpu.VMEM((NP, PAIR, W), F32),
            pltpu.VMEM((1, SUB), F32),
            pltpu.VMEM((CH, 128), F32),
            pltpu.VMEM((SUB, FF), BF16),
            pltpu.VMEM((NC, MAIN, W), BF16),
            pltpu.VMEM((NZ, NX * REST, W), BF16),
            pltpu.VMEM((NZ, NX * REST, W), BF16),
            pltpu.VMEM((NX, NZ * REST, W), BF16),
            pltpu.VMEM((NX, NZ * REST, W), BF16),
            pltpu.VMEM((NX * REST, W), F32),
            pltpu.VMEM((NX, NZ * REST, W), F32),
            pltpu.VMEM((1, 128), F32),
            pltpu.VMEM((NC, 1, 128), F32),
            pltpu.VMEM((NC, SUB, 128), F32),
            pltpu.VMEM((NC, CH, 128), F32),
            pltpu.VMEM((NL, CH, 128), F32),
            pltpu.VMEM((NZ, CH, 128), F32),
            pltpu.VMEM((NL, CH, 128), F32),
            pltpu.VMEM((NC, CH, 128), F32),
            pltpu.VMEM((NL, 1, 128), F32),
            pltpu.VMEM((NZ, 1, 128), F32),
            dma, dma, dma((2,)), dma((NC,)), dma((NC,)), dma((NC,)), dma((NC,)),
            dma((NZ,)), dma((NZ,)), dma((NX,)), dma((NX,)), dma((5,)), dma((5,)),
        ],
        compiler_params=pltpu.CompilerParams(
            collective_id=0, has_side_effects=True, vmem_limit_bytes=28 * 2**20
        ),
        cost_estimate=pl.CostEstimate(
            flops=8 * SUB * FF, bytes_accessed=4 * SUB * FF, transcendentals=0
        ),
        name="gather_kernel",
    )(*[pltpu.with_memory_space_constraint(a, pltpu.HBM) for a in arrays])
    new_weights, colm, rowm = pl.pallas_call(
        write_kernel,
        out_shape=(
            jax.ShapeDtypeStruct((NP, PAIR, W), F32),
            jax.ShapeDtypeStruct((CH, 128), F32),
            jax.ShapeDtypeStruct((1, SUB), F32),
        ),
        in_specs=[vmem] * 3,
        out_specs=(hbm,) * 3,
        scratch_shapes=[dma((3,))],
        compiler_params=pltpu.CompilerParams(vmem_limit_bytes=2**20),
        cost_estimate=pl.CostEstimate(
            flops=2 * SUB * FF, bytes_accessed=4 * SUB * FF, transcendentals=0
        ),
        name="write_kernel",
    )(done, colm, rowm)
    return (new_weights.reshape(SUB * NC, W), rowm.reshape(SUB), colm.reshape(W))


def solution(mesh):
    in_specs = (P(("row", "col"), None), P("row", "col"), P(("row", "col")), P("col"))
    out_specs = (P("row", "col"), P(("row", "col")), P("col"))
    return jax.shard_map(local, mesh=mesh, in_specs=in_specs, out_specs=out_specs, check_vma=False)
```
